32 devices in a mesh: groups: 2 (over y), expert: 4 (over z), dp: 4 (over x, core).
Axes of the slice: x: 2, y: 2, z: 4, core: 2. Of those that a mesh axis runs over, the one named last changes fastest.
Arguments:
- tokens: bfloat16 [4096, 1024], P(('groups', 'expert', 'dp')), parts along dimension 0, may hold values from -6 to 6
- cotangent: bfloat16 [4096, 1024], P(('groups', 'expert', 'dp')), parts along dimension 0, may hold values from -6 to 6
- expert_ids: int32 [4096, 2], P(('groups', 'expert', 'dp')), parts along dimension 0, may hold values from 0 to 3, all different within a row; in each aligned block of 128 rows (0 to 127, 128 to 255, ...) at most 80 rows name the same one
- gates: bfloat16 [4096, 2], P(('groups', 'expert', 'dp')), parts along dimension 0, may hold values from 0.049804688 to 1
- expert_in: bfloat16 [4, 1024, 2048], P('expert', None, 'dp'), may hold values from -0.1875 to 0.1875
- expert_out: bfloat16 [4, 2048, 1024], P('expert', 'dp'), may hold values from -0.125 to 0.125
Outputs:
- grad_tokens: bfloat16 [4096, 1024], P(('groups', 'expert', 'dp')), parts along dimension 0
- grad_gates: bfloat16 [4096, 2], P(('groups', 'expert', 'dp')), parts along dimension 0
- grad_in: bfloat16 [8, 1024, 2048], P(('groups', 'expert'), None, 'dp'), parts along dimension 0
- grad_out: bfloat16 [8, 2048, 1024], P(('groups', 'expert'), 'dp'), parts along dimension 0
The draws below stay inside these ranges and needn't reach their ends.
There are 2 independent parts, one for each index of `groups`. The reference program is written for one: setup_inputs(seed, part) draws one part's arguments, and reference() takes and returns one part's arrays. A program takes and returns all parts, laid end to end along the dimension named above; an argument that names none is the same for every part. Nothing has to cross between parts.
Inputs may be any that keep to these rules, and one draw needn't show every extreme that they name: `expert_ids`: the 2 experts of a token differ. Among the tokens of one device, at most 80 assignments name any one expert, and in every draw some device's tokens name some expert exactly 80 times.
All inputs are finite; a program needn't handle non-finite values.
Results may differ from the reference program's by a relative error of at most 0.0059.
Values may be sent and summed in bfloat16 or wider, within the bound.
A program may use at most 64 MiB of HBM per device.

```python
import math
import jax
import jax.numpy as jnp
import numpy as np
from jax import lax

D = 1024
FF = 2048
TOP = 2
TOK_DEV = 128
EXPERTS = 4
CAP = 80
TOKENS = 2048
N_EXPERT = 4
N_DP = 4


def steps_of(rng, extent, shards, low, largest):
    level, own = 1.0, jax.random.fold_in(rng, 6)
    for position, shards_of in shards:
        steps = jnp.exp(jax.random.uniform(jax.random.fold_in(own, position), (shards_of,), jnp.float32, low / len(shards), largest / len(shards)))
        level = level * jnp.repeat(steps, extent[position] // shards_of).reshape([-1 if axis == position else 1 for axis in range(len(extent))])
    return level


def routed_block(stream_key, own, number, rows, number_of, top, bound, lean):
    ranking = jax.random.permutation(stream_key, number_of)
    crowded, usual = portions_of(number_of, rows * top, bound, lean, True), portions_of(number_of, rows * top, bound, lean, False)
    places = jnp.arange(number_of)

    def named(tallies, turn):
        used = int((tallies > 0).sum())
        fixed = max(1, used // 4)
        moved = fixed + (places - fixed + turn * (used - fixed)) % max(1, number_of - fixed)
        return jnp.zeros((number_of,), jnp.int32).at[ranking[jnp.where(places < fixed, places, moved)]].set(jnp.asarray(tallies, jnp.int32))

    tallies = jnp.where(number % 4 == 0, named(crowded, number // 4), named(usual, number - number // 4 - 1))
    mixed = jax.random.permutation(jax.random.fold_in(own, 3), number_of)
    donor, receiver = mixed[0:number_of // 2 * 2:2], mixed[1:number_of // 2 * 2:2]
    slack = jnp.minimum(tallies[donor] - 1, bound - tallies[receiver]) // 2
    slack = jnp.where((donor == ranking[0]) | (receiver == ranking[0]) | (tallies[receiver] == 0), 0, jnp.maximum(slack, 0))
    moved = jax.random.randint(jax.random.fold_in(own, 4), (number_of // 2,), 0, 1 << 20) % (slack + 1)
    tallies = tallies.at[donor].add(-moved).at[receiver].add(moved)
    labels = jnp.searchsorted(jnp.cumsum(tallies), jnp.arange(rows * top), side="right").astype(jnp.int32)
    listing = labels.reshape(top, rows).T
    listing = listing[jax.random.permutation(jax.random.fold_in(own, 1), rows)]
    turn = jax.random.randint(jax.random.fold_in(own, 2), (rows, 1), 0, top)
    return jnp.take_along_axis(listing, (jnp.arange(top)[None, :] + turn) % top, axis=1)


def portions_of(amount, total, most, slope, full):
    weights = [(1 << 20) // math.isqrt(grade ** slope) + 1 for grade in range(1, amount + 1)]
    largest = most if full else min(most, max(-(-total // amount), total * weights[0] // sum(weights)))
    least = 1 if total - largest >= amount - 1 else 0
    holding, rest = [largest] + [least] * (amount - 1), total - largest - least * (amount - 1)
    while rest > 0:
        candidates = [i for i in range(1, amount) if holding[i] < largest] or [i for i in range(1, amount) if holding[i] < most]
        whole, remaining = sum([weights[i] for i in candidates]), rest
        for i in candidates:
            extra = min(most - holding[i], max(1, remaining * weights[i] // whole), rest)
            holding[i] = holding[i] + extra
            rest = rest - extra
    return np.array(holding)


def centred(rng, shape, spread, most, shards=(), held_as=jnp.bfloat16):
    factor_of = steps_of(rng, shape, shards, -0.22, 0.18) if shards else 1.0
    values = jax.random.normal(rng, shape, jnp.float32) * spread * factor_of
    return jnp.minimum(jnp.maximum(values, -most), most).astype(held_as)


def setup_inputs(seed: int = 0, part: int = 0) -> dict:
    arg_keys = jax.random.split(jax.random.key(seed), 7)
    part_keys = jax.random.split(jax.random.fold_in(arg_keys[6], part), 7)
    tokens = centred(part_keys[0], (TOKENS, D), 1.0, 6.0, ((0, 16),))
    cotangent = centred(part_keys[1], (TOKENS, D), 1.0, 6.0, ((0, 16),))
    expert_ids_keys = jax.random.split(jax.random.fold_in(part_keys[2], 1), TOKENS // TOK_DEV)
    expert_ids_turns = jax.random.permutation(jax.random.fold_in(part_keys[2], 3), TOKENS // TOK_DEV)
    expert_ids = jax.vmap(lambda own, number: routed_block(jax.random.fold_in(part_keys[2], 2), own, number, TOK_DEV, EXPERTS, TOP, CAP, 2))(expert_ids_keys, expert_ids_turns).reshape((TOKENS, TOP))
    gates = jnp.clip(jnp.exp(math.log(1.0) - 2.9996462 * jax.random.uniform(part_keys[3], (TOKENS, TOP), jnp.float32) ** steps_of(part_keys[3], (TOKENS, TOP), ((0, 16),), -0.2, 0.2)), 0.049804688, 1.0).astype(jnp.bfloat16)
    expert_in = centred(arg_keys[4], (EXPERTS, D, FF), D ** -0.5, 0.1875, ((0, 4), (2, 4)))
    expert_out = centred(arg_keys[5], (EXPERTS, FF, D), FF ** -0.5, 0.125, ((0, 4), (1, 4)))
    return {"tokens": tokens, "cotangent": cotangent, "expert_ids": expert_ids, "gates": gates, "expert_in": expert_in, "expert_out": expert_out}


def expert_pass(operands):
    rows_x, rows_g, rows_p, weight_in, weight_out = operands
    pre_act = jnp.dot(rows_x, weight_in, preferred_element_type=jnp.float32)
    activated, pullback = jax.vjp(jax.nn.gelu, pre_act)
    grad_act = jnp.dot(rows_g, weight_out.T, preferred_element_type=jnp.float32)
    gate_part = lax.optimization_barrier(jnp.sum(activated * grad_act, axis=1))
    gate_scale = rows_p[:, None]
    hidden_grad = pullback(gate_scale * grad_act)[0].astype(jnp.bfloat16)
    scaled_act = (gate_scale * activated).astype(jnp.bfloat16)
    grad_first = jnp.dot(rows_x.T, hidden_grad, preferred_element_type=jnp.float32).astype(jnp.bfloat16)
    grad_second = jnp.dot(scaled_act.T, rows_g, preferred_element_type=jnp.float32).astype(jnp.bfloat16)
    row_grads = jnp.dot(hidden_grad, weight_in.T, preferred_element_type=jnp.float32).astype(jnp.bfloat16)
    return (grad_first, grad_second, row_grads, gate_part)

def reference(tokens, cotangent, expert_ids, gates, expert_in, expert_out):
    dev_count = N_EXPERT * N_DP
    ids = expert_ids.reshape(dev_count, TOP * TOK_DEV)
    onehot = (ids[:, :, None] == jnp.arange(EXPERTS, dtype=jnp.int32)[None, None, :]).astype(jnp.int32)
    rank = lax.optimization_barrier(jnp.sum((jnp.cumsum(onehot, axis=1) - onehot) * onehot, axis=2))
    slot_of = (jnp.arange(dev_count, dtype=jnp.int32)[:, None] * CAP + rank).reshape(-1)
    expert_of = ids.reshape(-1)
    row_total = dev_count * CAP
    assign_count = TOKENS * TOP
    owner = jnp.full((EXPERTS, row_total), assign_count, jnp.int32)
    owner = owner.at[expert_of, slot_of].set(jnp.arange(assign_count, dtype=jnp.int32))
    token_of = jnp.where(owner < assign_count, owner // TOP, TOKENS).astype(jnp.int32)
    padded_x = jnp.concatenate([tokens, jnp.zeros((1, D), tokens.dtype)], axis=0)
    padded_g = jnp.concatenate([cotangent, jnp.zeros((1, D), cotangent.dtype)], axis=0)
    padded_p = jnp.concatenate([gates.reshape(-1).astype(jnp.float32), jnp.zeros((1,), jnp.float32)], axis=0)
    buffer_x = padded_x[token_of]
    buffer_g = padded_g[token_of]
    buffer_p = padded_p[owner]
    grad_in, grad_out, row_grads, gate_part = lax.map(expert_pass, (buffer_x, buffer_g, buffer_p, expert_in, expert_out))
    picked = row_grads[expert_of, slot_of].astype(jnp.float32).reshape(TOKENS, TOP, D)
    grad_tokens = lax.optimization_barrier(jnp.sum(picked, axis=1)).astype(jnp.bfloat16)
    grad_gates = gate_part[expert_of, slot_of].astype(jnp.bfloat16).reshape(TOKENS, TOP)
    return (grad_tokens, grad_gates, grad_in, grad_out)
```

```python
import functools

import jax
import jax.numpy as jnp
from jax import lax
from jax.experimental import pallas as pl
from jax.experimental.pallas import tpu as pltpu
from jax.sharding import PartitionSpec as P

F32 = jnp.float32
BF16 = jnp.bfloat16


def dot(a, b, ca, cb):
    return lax.dot_general(a, b, (((ca,), (cb,)), ((), ())), preferred_element_type=F32)


def split(v):
    hi = v.astype(BF16)
    return hi, (v - hi.astype(F32)).astype(BF16)


def gelu_both(v):
    k = 0.7978845608028654
    v2 = v * v
    t = jnp.tanh(k * v * (1.0 + 0.044715 * v2))
    half = 0.5 + 0.5 * t
    act = v * half
    slope = half + act * (1.0 - t) * (k * (1.0 + 3.0 * 0.044715 * v2))
    return act, slope


def kernel(
    n_exp, n_dp, cap, width, hid,
    ids_ref, gate_ref, tok_ref, cot_ref, win_hbm, wout_hbm,
    gtok_ref, ggate_ref, gin_ref, gout_ref,
    win, wout, hit_s, rank_s, placed, send, buf, h_buf, a_buf,
    part, sib_in, x_out, x_in, own_sum, z_out, back, g_part, g_in, g_out, g_back,
    w_sem, zs, zr, xs, xr, fs, fr, ps, pr, rs, rr, bs, br, gs, gr, ks, kr,
):
    nx = n_dp // 2
    me = lax.axis_index("expert")
    d = lax.axis_index("dp")
    c = d % 2
    x = d // 2
    tok_count = tok_ref.shape[0]
    lanes = placed.shape[1]
    chunk = n_dp * cap

    def exp_dev(e):
        return {"expert": e}

    def dp_dev(i):
        return {"dp": i}

    sib = x * 2 + (1 - c)

    def x_peer(i):
        return ((x + i) % nx) * 2 + c

    def up(s):
        return (me + s) % n_exp

    def down(s):
        return (me + n_exp - s) % n_exp

    def rows(s, who):
        return pl.ds(pl.multiple_of(s * chunk + who * cap, 16), cap)

    def rcopy(src, dst, ss, rsem, dev):
        return pltpu.make_async_remote_copy(
            src_ref=src, dst_ref=dst, send_sem=ss, recv_sem=rsem,
            device_id=dev, device_id_type=pl.DeviceIdType.MESH,
        )

    cw_in = pltpu.make_async_copy(win_hbm, win, w_sem.at[0])
    cw_out = pltpu.make_async_copy(wout_hbm, wout, w_sem.at[1])
    cw_in.start()
    cw_out.start()

    barrier = pltpu.get_barrier_semaphore()

    for s in range(1, n_exp):
        pl.semaphore_signal(barrier, inc=1, device_id=exp_dev(up(s)), device_id_type=pl.DeviceIdType.MESH)
    for i in range(1, n_dp):
        pl.semaphore_signal(
            barrier, inc=1, device_id=dp_dev((d + i) % n_dp), device_id_type=pl.DeviceIdType.MESH
        )

    ids0 = ids_ref[0:1, :]
    ids1 = ids_ref[1:2, :]
    p0 = gate_ref[0:1, :]
    p1 = gate_ref[1:2, :]
    e_rows = hit_s.shape[0]
    e_iota = lax.broadcasted_iota(jnp.int32, (e_rows, tok_count), 0)
    hit = jnp.where(e_iota == ids0, 1.0, 0.0) + jnp.where(e_iota == ids1, 1.0, 0.0)
    before = jnp.where(
        lax.broadcasted_iota(jnp.int32, (tok_count, tok_count), 0)
        < lax.broadcasted_iota(jnp.int32, (tok_count, tok_count), 1),
        1.0, 0.0,
    )
    rank = dot(hit.astype(BF16), before.astype(BF16), 1, 0)
    slot_iota = lax.broadcasted_iota(jnp.int32, (lanes, tok_count), 0).astype(F32)
    hit_s[...] = hit
    rank_s[...] = rank
    pl.semaphore_wait(barrier, n_exp - 1 + n_dp - 1)

    def z_copy(s, k):
        return rcopy(
            send.at[k, pl.ds(pl.multiple_of(s * cap, 16), cap)], buf.at[k, rows(s, d)],
            zs.at[k, s], zr.at[k, s], exp_dev(up(s)),
        )

    def x_copy(s, k, i):
        return rcopy(
            buf.at[k, rows(s, d)], buf.at[k, rows(s, d)],
            xs.at[k, s, i - 1], xr.at[k, s, i - 1], dp_dev(x_peer(i)),
        )

    def x_landed(s, k, i):
        who = ((x + nx - i) % nx) * 2 + c
        ref = buf.at[k, rows(s, who)]
        return rcopy(ref, ref, xs.at[k, s, i - 1], xr.at[k, s, i - 1], dp_dev(x_peer(i)))

    def f_copy(s, k, i, core):
        ref = buf.at[k, rows(s, ((x + nx - i) % nx) * 2 + core)]
        return rcopy(ref, ref, fs.at[k, s, i], fr.at[k, s, i], dp_dev(sib))

    def fill(s, k):
        e = up(s)
        h_row = hit_s[pl.ds(e, 1), :]
        r_row = rank_s[pl.ds(e, 1), :]
        here = jnp.where(slot_iota == r_row, h_row, 0.0)
        if k == 0:
            placed[pl.ds(pl.multiple_of(s * lanes, 16), lanes), :] = here.astype(BF16)
            return dot(here[:cap].astype(BF16), tok_ref[...], 1, 0).astype(BF16)
        p_row = jnp.where(ids0 == e, p0, p1)
        return dot((here[:cap] * p_row).astype(BF16), cot_ref[...], 1, 0).astype(BF16)

    def start_send(s):
        for k in range(2):
            send[k, pl.ds(pl.multiple_of(s * cap, 16), cap), :] = fill(s, k)
            z_copy(s, k).start()

    def spread(s, k):
        for i in range(1, nx):
            x_copy(s, k, i).start()
        f_copy(s, k, 0, c).start()

    def f1(s):
        for k in range(2):
            z_copy(s, k).wait_recv()
            spread(s, k)

    def f2(s):
        for k in range(2):
            for i in range(1, nx):
                x_landed(s, k, i).wait_recv()
                f_copy(s, k, i, c).start()

    def p_copy(s, i):
        who = ((x + i) % nx) * 2 + (1 - c)
        return rcopy(
            part.at[rows(s, who)], sib_in.at[s, i], ps.at[s, i], pr.at[s, i], dp_dev(sib)
        )

    def compute(s):
        for k in range(2):
            for i in range(nx):
                f_copy(s, k, i, 1 - c).wait_recv()
        here = pl.ds(pl.multiple_of(s * chunk, 16), chunk)
        pre = dot(buf[0, here, :], win[...], 1, 0)
        grad_act = dot(buf[1, here, :], wout[...], 1, 1)
        act, slope = gelu_both(pre)
        hidden = (grad_act * slope).astype(BF16)
        h_buf[here, :] = hidden
        a_buf[here, :] = act.astype(BF16)
        part[here, :] = dot(hidden, win[...], 1, 1).astype(BF16)
        for i in range(nx):
            p_copy(s, i).start()
        hi, lo = split(act * grad_act)
        ones = jnp.ones((8, hid), BF16)
        for i in range(n_dp):
            own = slice(i * cap, (i + 1) * cap)
            g_part[i, s, :, 0:cap] = dot(ones, hi[own], 1, 1) + dot(ones, lo[own], 1, 1)

    def r_copy(s, i):
        return rcopy(
            x_out.at[s, i - 1], x_in.at[s, i - 1], rs.at[s, i - 1], rr.at[s, i - 1], dp_dev(x_peer(i))
        )

    def r1(s):
        for i in list(range(1, nx)) + [0]:
            p_copy(s, i).wait_recv()
            who = ((x + i) % nx) * 2 + c
            total = part[rows(s, who), :].astype(F32) + sib_in[s, i].astype(F32)
            if i == 0:
                own_sum[s] = total
            else:
                x_out[s, i - 1] = total.astype(BF16)
                r_copy(s, i).start()

    def b_copy(s):
        return rcopy(
            z_out.at[s], back.at[pl.ds(pl.multiple_of(s * cap, 16), cap)],
            bs.at[s], br.at[s], exp_dev(down(s)),
        )

    def r2(s):
        total = own_sum[s]
        for i in range(1, nx):
            r_copy(s, i).wait_recv()
            total += x_in[s, i - 1].astype(F32)
        return total.astype(BF16)

    def r2_send(s):
        z_out[s] = r2(s)
        b_copy(s).start()

    def g_copy(i):
        return rcopy(
            g_part.at[(d + i) % n_dp], g_in.at[i - 1], gs.at[i - 1], gr.at[i - 1],
            dp_dev((d + i) % n_dp),
        )

    def k_copy(s):
        return rcopy(g_out.at[s], g_back.at[s], ks.at[s], kr.at[s], exp_dev(down(s)))

    g_part[...] = jnp.zeros_like(g_part)
    unroll = n_exp <= 4

    def over(low, high, body):
        if unroll:
            for s in range(low, high):
                body(s)
        else:
            lax.fori_loop(low, high, lambda s, t: (body(s), t)[1], 0)

    for k in range(2):
        buf[k, rows(0, d), :] = fill(0, k)
        spread(0, k)
    over(1, n_exp, start_send)
    cw_in.wait()
    cw_out.wait()

    f1(1)
    f2(0)
    compute(0)
    f1(2)
    f2(1)
    compute(1)
    r1(0)

    def steady(t):
        f1(t)
        f2(t - 1)
        compute(t - 1)
        r1(t - 2)

        if unroll and t == 3:
            back[0:cap, :] = r2(0)
        else:
            r2_send(t - 3)

    if unroll:
        over(3, n_exp, steady)
    else:
        f1(3)
        f2(2)
        compute(2)
        r1(1)
        back[0:cap, :] = r2(0)
        over(4, n_exp, steady)
    last = n_exp - 1
    f2(last)
    compute(last)
    for i in range(1, n_dp):
        g_copy(i).start()
    r1(last - 1)
    r2_send(last - 2)
    tile = 256

    def in_tile(j, t):
        cols = pl.ds(pl.multiple_of(j * tile, tile), tile)
        gin_ref[cols, :] = dot(buf[0, :, cols], h_buf[...], 0, 0).astype(BF16)
        return t

    def out_tile(j, t):
        cols = pl.ds(pl.multiple_of(j * tile, tile), tile)
        gout_ref[:, cols] = dot(a_buf[...], buf[1, :, cols], 0, 0).astype(BF16)
        return t

    r1(last)
    r2_send(last - 1)
    lax.fori_loop(0, width // tile, in_tile, 0)
    r2_send(last)
    g_sum = g_part[d]
    for i in range(1, n_dp):
        g_copy(i).wait_recv()
        g_sum += g_in[i - 1]
    g_out[...] = g_sum
    over(1, n_exp, lambda s: k_copy(s).start())
    lax.fori_loop(0, width // tile, out_tile, 0)
    g_back[0] = g_out[0]
    over(1, n_exp, lambda s: k_copy(s).wait_recv())
    gate0 = jnp.zeros((8, tok_count), F32)
    gate1 = jnp.zeros((8, tok_count), F32)
    for s in range(n_exp):
        hi, lo = split(g_back[s])
        mine = placed[s * lanes : (s + 1) * lanes, :]
        value = dot(hi, mine, 1, 0) + dot(lo, mine, 1, 0)
        gate0 += jnp.where(ids0 == up(s), value, 0.0)
        gate1 += jnp.where(ids1 == up(s), value, 0.0)
    ggate_ref[0:8, :] = gate0 / p0
    ggate_ref[8:16, :] = gate1 / p1

    over(1, n_exp, lambda s: b_copy(s).wait_recv())
    total = jnp.zeros((tok_count, width), F32)
    for s in range(n_exp):
        total += dot(
            placed[s * lanes : s * lanes + cap, :], back[s * cap : (s + 1) * cap, :], 0, 0
        )
    gtok_ref[...] = total.astype(BF16)

    def drain(s):
        for k in range(2):
            z_copy(s, k).wait_send()
        b_copy(s).wait_send()
        k_copy(s).wait_send()

    def drain_all(s):
        for k in range(2):
            for i in range(1, nx):
                x_copy(s, k, i).wait_send()
            for i in range(nx):
                f_copy(s, k, i, c).wait_send()
        for i in range(nx):
            p_copy(s, i).wait_send()
        for i in range(1, nx):
            r_copy(s, i).wait_send()

    over(1, n_exp, drain)
    over(0, n_exp, drain_all)
    for i in range(1, n_dp):
        g_copy(i).wait_send()


def per_device(tokens, cotangent, expert_ids, gates, expert_in, expert_out):
    tok_count, width = tokens.shape
    n_exp = lax.axis_size("expert")
    n_dp = lax.axis_size("dp")
    nx = n_dp // 2
    hid = expert_in.shape[2]
    cap = (5 * tok_count + 2 * n_exp - 1) // (2 * n_exp)
    cap = (cap + 15) // 16 * 16
    chunk = n_dp * cap
    lanes = 128
    e_rows = (n_exp + 15) // 16 * 16
    vmem = pl.BlockSpec(memory_space=pltpu.VMEM)
    hbm = pl.BlockSpec(memory_space=pl.ANY)
    dma = pltpu.SemaphoreType.DMA
    far = max(nx - 1, 1)
    grad_tokens, gate_rows, grad_in, grad_out = pl.pallas_call(
        functools.partial(kernel, n_exp, n_dp, cap, width, hid),
        out_shape=(
            jax.ShapeDtypeStruct((tok_count, width), BF16),
            jax.ShapeDtypeStruct((16, tok_count), F32),
            jax.ShapeDtypeStruct((width, hid), BF16),
            jax.ShapeDtypeStruct((hid, width), BF16),
        ),
        in_specs=[vmem] * 4 + [hbm] * 2,
        out_specs=(vmem,) * 4,
        scratch_shapes=[
            pltpu.VMEM((width, hid), BF16),
            pltpu.VMEM((hid, width), BF16),
            pltpu.VMEM((e_rows, tok_count), F32),
            pltpu.VMEM((e_rows, tok_count), F32),
            pltpu.VMEM((n_exp * lanes, tok_count), BF16),
            pltpu.VMEM((2, n_exp * cap, width), BF16),
            pltpu.VMEM((2, n_exp * chunk, width), BF16),
            pltpu.VMEM((n_exp * chunk, hid), BF16),
            pltpu.VMEM((n_exp * chunk, hid), BF16),
            pltpu.VMEM((n_exp * chunk, width), BF16),
            pltpu.VMEM((n_exp, nx, cap, width), BF16),
            pltpu.VMEM((n_exp, far, cap, width), BF16),
            pltpu.VMEM((n_exp, far, cap, width), BF16),
            pltpu.VMEM((n_exp, cap, width), F32),
            pltpu.VMEM((n_exp, cap, width), BF16),
            pltpu.VMEM((n_exp * cap, width), BF16),
            pltpu.VMEM((n_dp, n_exp, 8, lanes), F32),
            pltpu.VMEM((n_dp - 1, n_exp, 8, lanes), F32),
            pltpu.VMEM((n_exp, 8, lanes), F32),
            pltpu.VMEM((n_exp, 8, lanes), F32),
            dma((2,)),
            dma((2, n_exp)), dma((2, n_exp)),
            dma((2, n_exp, far)), dma((2, n_exp, far)),
            dma((2, n_exp, nx)), dma((2, n_exp, nx)),
            dma((n_exp, nx)), dma((n_exp, nx)),
            dma((n_exp, far)), dma((n_exp, far)),
            dma((n_exp,)), dma((n_exp,)),
            dma((n_dp - 1,)), dma((n_dp - 1,)),
            dma((n_exp,)), dma((n_exp,)),
        ],
        compiler_params=pltpu.CompilerParams(
            collective_id=0, has_side_effects=True, vmem_limit_bytes=60 * 1024 * 1024
        ),
    )(
        expert_ids.T, gates.T.astype(F32), tokens, cotangent, expert_in[0], expert_out[0]
    )
    grad_gates = gate_rows[0::8].T.astype(BF16)
    return grad_tokens, grad_gates, grad_in[None], grad_out[None]


def solution(mesh):
    rows = P(("groups", "expert", "dp"), None)
    return jax.shard_map(
        per_device,
        mesh=mesh,
        in_specs=(rows, rows, rows, rows, P("expert", None, "dp"), P("expert", "dp", None)),
        out_specs=(
            rows,
            rows,
            P(("groups", "expert"), None, "dp"),
            P(("groups", "expert"), "dp", None),
        ),
        check_vma=False,
    )
```

```python
import functools

import jax
import jax.numpy as jnp
from jax import lax
from jax.experimental import pallas as pl
from jax.experimental.pallas import tpu as pltpu
from jax.sharding import PartitionSpec as P

F32 = jnp.float32
BF16 = jnp.bfloat16


def dot(a, b, ca, cb):
    return lax.dot_general(a, b, (((ca,), (cb,)), ((), ())), preferred_element_type=F32)


def split(v):
    hi = v.astype(BF16)
    return hi, (v - hi.astype(F32)).astype(BF16)


def gelu_both(v):
    k = 0.7978845608028654
    v2 = v * v
    t = jnp.tanh(k * v * (1.0 + 0.044715 * v2))
    half = 0.5 + 0.5 * t
    act = v * half
    slope = half + act * (1.0 - t) * (k * (1.0 + 3.0 * 0.044715 * v2))
    return act, slope


def kernel(
    n_exp, n_dp, cap, width, hid,
    ids_ref, gate_ref, tok_ref, cot_ref, win_hbm, wout_hbm,
    gtok_ref, ggate_ref, gin_ref, gout_ref,
    win, wout, hit_s, rank_s, placed, send, buf, h_buf, a_buf,
    part, sib_in, x_out, x_in, own_sum, z_out, back, g_part, g_in, g_out, g_back,
    w_sem, zs, zr, xs, xr, fs, fr, ps, pr, rs, rr, bs, br, gs, gr, ks, kr,
):
    nx = n_dp // 2
    me = lax.axis_index("expert")
    d = lax.axis_index("dp")
    c = d % 2
    x = d // 2
    tok_count = tok_ref.shape[0]
    lanes = placed.shape[1]
    chunk = n_dp * cap

    def exp_dev(e):
        return {"expert": e}

    def dp_dev(i):
        return {"dp": i}

    sib = x * 2 + (1 - c)

    def x_peer(i):
        return ((x + i) % nx) * 2 + c

    def up(s):
        return (me + s) % n_exp

    def down(s):
        return (me + n_exp - s) % n_exp

    def rows(s, who):
        return pl.ds(pl.multiple_of(s * chunk + who * cap, 16), cap)

    def rcopy(src, dst, ss, rsem, dev):
        return pltpu.make_async_remote_copy(
            src_ref=src, dst_ref=dst, send_sem=ss, recv_sem=rsem,
            device_id=dev, device_id_type=pl.DeviceIdType.MESH,
        )

    cw_in = pltpu.make_async_copy(win_hbm, win, w_sem.at[0])
    cw_out = pltpu.make_async_copy(wout_hbm, wout, w_sem.at[1])
    cw_in.start()
    cw_out.start()

    barrier = pltpu.get_barrier_semaphore()

    for s in range(1, n_exp):
        pl.semaphore_signal(barrier, inc=1, device_id=exp_dev(up(s)), device_id_type=pl.DeviceIdType.MESH)
    for i in range(1, n_dp):
        pl.semaphore_signal(
            barrier, inc=1, device_id=dp_dev((d + i) % n_dp), device_id_type=pl.DeviceIdType.MESH
        )

    ids0 = ids_ref[0:1, :]
    ids1 = ids_ref[1:2, :]
    both = gate_ref[...].astype(F32)
    p0 = both[0:1, :]
    p1 = both[1:2, :]
    e_rows = hit_s.shape[0]
    e_iota = lax.broadcasted_iota(jnp.int32, (e_rows, tok_count), 0)
    hit = jnp.where(e_iota == ids0, 1.0, 0.0) + jnp.where(e_iota == ids1, 1.0, 0.0)
    before = jnp.where(
        lax.broadcasted_iota(jnp.int32, (tok_count, tok_count), 0)
        < lax.broadcasted_iota(jnp.int32, (tok_count, tok_count), 1),
        1.0, 0.0,
    )
    rank = dot(hit.astype(BF16), before.astype(BF16), 1, 0)
    slot_iota = lax.broadcasted_iota(jnp.int32, (lanes, tok_count), 0).astype(F32)
    hit_s[...] = hit
    rank_s[...] = rank
    pl.semaphore_wait(barrier, n_exp - 1 + n_dp - 1)

    def z_copy(s, k):
        return rcopy(
            send.at[k, pl.ds(pl.multiple_of(s * cap, 16), cap)], buf.at[k, rows(s, d)],
            zs.at[k, s], zr.at[k, s], exp_dev(up(s)),
        )

    def x_copy(s, k, i):
        return rcopy(
            buf.at[k, rows(s, d)], buf.at[k, rows(s, d)],
            xs.at[k, s, i - 1], xr.at[k, s, i - 1], dp_dev(x_peer(i)),
        )

    def x_landed(s, k, i):
        who = ((x + nx - i) % nx) * 2 + c
        ref = buf.at[k, rows(s, who)]
        return rcopy(ref, ref, xs.at[k, s, i - 1], xr.at[k, s, i - 1], dp_dev(x_peer(i)))

    def f_copy(s, k, i, core):
        ref = buf.at[k, rows(s, ((x + nx - i) % nx) * 2 + core)]
        return rcopy(ref, ref, fs.at[k, s, i], fr.at[k, s, i], dp_dev(sib))

    def fill(s, k):
        e = up(s)
        h_row = hit_s[pl.ds(e, 1), :]
        r_row = rank_s[pl.ds(e, 1), :]
        here = jnp.where(slot_iota == r_row, h_row, 0.0)
        if k == 0:
            placed[pl.ds(pl.multiple_of(s * lanes, 16), lanes), :] = here.astype(BF16)
            return dot(here[:cap].astype(BF16), tok_ref[...], 1, 0).astype(BF16)
        p_row = jnp.where(ids0 == e, p0, p1)
        return dot((here[:cap] * p_row).astype(BF16), cot_ref[...], 1, 0).astype(BF16)

    def start_send(s):
        for k in range(2):
            send[k, pl.ds(pl.multiple_of(s * cap, 16), cap), :] = fill(s, k)
            if unroll and 2 * (s - 1) + k < ahead:
                z_copy(s, k).start()
            elif not unroll:
                pl.when(2 * (s - 1) + k < ahead)(lambda: z_copy(s, k).start())

    def spread(s, k):
        for i in range(1, nx):
            x_copy(s, k, i).start()
        f_copy(s, k, 0, c).start()

    def kick(s, k):
        z_copy(s, k).wait_send()
        later = s + (k + ahead) // 2
        if unroll and later < n_exp:
            z_copy(later, (k + ahead) % 2).start()
        elif not unroll:
            pl.when(later < n_exp)(lambda: z_copy(later, (k + ahead) % 2).start())

    def f1(s):
        for k in range(2):
            kick(s, k)
            z_copy(s, k).wait_recv()
            spread(s, k)

    def f2(s):
        for k in range(2):
            for i in range(1, nx):
                x_landed(s, k, i).wait_recv()
                f_copy(s, k, i, c).start()

    def p_copy(s, i):
        who = ((x + i) % nx) * 2 + (1 - c)
        return rcopy(
            part.at[rows(s, who)], sib_in.at[s, i], ps.at[s, i], pr.at[s, i], dp_dev(sib)
        )

    def compute(s):
        for k in range(2):
            for i in range(nx):
                f_copy(s, k, i, 1 - c).wait_recv()
        here = pl.ds(pl.multiple_of(s * chunk, 16), chunk)
        pre = dot(buf[0, here, :], win[...], 1, 0)
        grad_act = dot(buf[1, here, :], wout[...], 1, 1)
        act, slope = gelu_both(pre)
        hidden = (grad_act * slope).astype(BF16)
        h_buf[here, :] = hidden
        a_buf[here, :] = act.astype(BF16)
        part[here, :] = dot(hidden, win[...], 1, 1).astype(BF16)
        for i in range(nx):
            p_copy(s, i).start()
        hi, lo = split(act * grad_act)
        ones = jnp.ones((8, hid), BF16)
        for i in range(n_dp):
            own = slice(i * cap, (i + 1) * cap)
            g_part[i, s, :, 0:cap] = dot(ones, hi[own], 1, 1) + dot(ones, lo[own], 1, 1)

    def r_copy(s, i):
        return rcopy(
            x_out.at[s, i - 1], x_in.at[s, i - 1], rs.at[s, i - 1], rr.at[s, i - 1], dp_dev(x_peer(i))
        )

    def r1(s):
        for i in list(range(1, nx)) + [0]:
            p_copy(s, i).wait_recv()
            who = ((x + i) % nx) * 2 + c
            total = part[rows(s, who), :].astype(F32) + sib_in[s, i].astype(F32)
            if i == 0:
                own_sum[s] = total
            else:
                x_out[s, i - 1] = total.astype(BF16)
                r_copy(s, i).start()

    def b_copy(s):
        return rcopy(
            z_out.at[s], back.at[pl.ds(pl.multiple_of(s * cap, 16), cap)],
            bs.at[s], br.at[s], exp_dev(down(s)),
        )

    def r2(s):
        total = own_sum[s]
        for i in range(1, nx):
            r_copy(s, i).wait_recv()
            total += x_in[s, i - 1].astype(F32)
        return total.astype(BF16)

    def r2_send(s):
        z_out[s] = r2(s)
        b_copy(s).start()

    def g_copy(i):
        return rcopy(
            g_part.at[(d + i) % n_dp], g_in.at[i - 1], gs.at[i - 1], gr.at[i - 1],
            dp_dev((d + i) % n_dp),
        )

    def k_copy(s):
        return rcopy(g_out.at[s], g_back.at[s], ks.at[s], kr.at[s], exp_dev(down(s)))

    g_part[...] = jnp.zeros_like(g_part)
    unroll = n_exp == 4
    ahead = 1

    def over(low, high, body):
        if unroll:
            for s in range(low, high):
                body(s)
        else:
            lax.fori_loop(low, high, lambda s, t: (body(s), t)[1], 0)

    for k in range(2):
        buf[k, rows(0, d), :] = fill(0, k)
        spread(0, k)
    over(1, n_exp, start_send)
    cw_in.wait()
    cw_out.wait()

    if unroll:
        f1(1)
        f2(0)
        f1(2)
        f2(1)
        compute(0)
        f1(3)
        f2(2)
        compute(1)
        r1(0)
        compute(2)
        r1(1)
        back[0:cap, :] = r2(0)
    else:
        f1(1)
        f2(0)
        compute(0)
        f1(2)
        f2(1)
        compute(1)
        r1(0)
        f1(3)
        f2(2)
        compute(2)
        r1(1)
        back[0:cap, :] = r2(0)

        def steady(t):
            f1(t)
            f2(t - 1)
            compute(t - 1)
            r1(t - 2)
            r2_send(t - 3)

        over(4, n_exp, steady)
    last = n_exp - 1
    f2(last)
    compute(last)
    for i in range(1, n_dp):
        g_copy(i).start()
    r1(last - 1)
    r2_send(last - 2)
    tile = 256

    def in_tile(j, t):
        cols = pl.ds(pl.multiple_of(j * tile, tile), tile)
        gin_ref[cols, :] = dot(buf[0, :, cols], h_buf[...], 0, 0).astype(BF16)
        return t

    def out_tile(j, t):
        cols = pl.ds(pl.multiple_of(j * tile, tile), tile)
        gout_ref[:, cols] = dot(a_buf[...], buf[1, :, cols], 0, 0).astype(BF16)
        return t

    r1(last)
    r2_send(last - 1)
    lax.fori_loop(0, width // tile, in_tile, 0)
    r2_send(last)
    g_sum = g_part[d]
    for i in range(1, n_dp):
        g_copy(i).wait_recv()
        g_sum += g_in[i - 1]
    g_out[...] = g_sum
    over(1, n_exp, lambda s: k_copy(s).start())
    lax.fori_loop(0, width // tile, out_tile, 0)
    g_back[0] = g_out[0]
    over(1, n_exp, lambda s: k_copy(s).wait_recv())
    gate0 = jnp.zeros((8, tok_count), F32)
    gate1 = jnp.zeros((8, tok_count), F32)
    for s in range(n_exp):
        hi, lo = split(g_back[s])
        mine = placed[s * lanes : (s + 1) * lanes, :]
        value = dot(hi, mine, 1, 0) + dot(lo, mine, 1, 0)
        gate0 += jnp.where(ids0 == up(s), value, 0.0)
        gate1 += jnp.where(ids1 == up(s), value, 0.0)
    first = lax.broadcasted_iota(jnp.int32, (2, tok_count), 0) == 0
    ggate_ref[...] = jnp.where(first, gate0[0:2] / p0, gate1[0:2] / p1).astype(BF16)

    over(1, n_exp, lambda s: b_copy(s).wait_recv())
    total = jnp.zeros((tok_count, width), F32)
    for s in range(n_exp):
        total += dot(
            placed[s * lanes : s * lanes + cap, :], back[s * cap : (s + 1) * cap, :], 0, 0
        )
    gtok_ref[...] = total.astype(BF16)

    def drain(s):
        b_copy(s).wait_send()
        k_copy(s).wait_send()

    def drain_all(s):
        for k in range(2):
            for i in range(1, nx):
                x_copy(s, k, i).wait_send()
            for i in range(nx):
                f_copy(s, k, i, c).wait_send()
        for i in range(nx):
            p_copy(s, i).wait_send()
        for i in range(1, nx):
            r_copy(s, i).wait_send()

    over(1, n_exp, drain)
    over(0, n_exp, drain_all)
    for i in range(1, n_dp):
        g_copy(i).wait_send()


def per_device(tokens, cotangent, expert_ids, gates, expert_in, expert_out):
    tok_count, width = tokens.shape
    n_exp = lax.axis_size("expert")
    n_dp = lax.axis_size("dp")
    nx = n_dp // 2
    hid = expert_in.shape[2]
    cap = (5 * tok_count + 2 * n_exp - 1) // (2 * n_exp)
    cap = (cap + 15) // 16 * 16
    chunk = n_dp * cap
    lanes = 128
    e_rows = (n_exp + 15) // 16 * 16
    vmem = pl.BlockSpec(memory_space=pltpu.VMEM)
    hbm = pl.BlockSpec(memory_space=pltpu.HBM)
    dma = pltpu.SemaphoreType.DMA
    far = max(nx - 1, 1)
    grad_tokens, gate_rows, grad_in, grad_out = pl.pallas_call(
        functools.partial(kernel, n_exp, n_dp, cap, width, hid),
        out_shape=(
            jax.ShapeDtypeStruct((tok_count, width), BF16),
            jax.ShapeDtypeStruct((2, tok_count), BF16),
            jax.ShapeDtypeStruct((width, hid), BF16),
            jax.ShapeDtypeStruct((hid, width), BF16),
        ),
        in_specs=[vmem] * 4 + [hbm] * 2,
        out_specs=(vmem,) * 4,
        scratch_shapes=[
            pltpu.VMEM((width, hid), BF16),
            pltpu.VMEM((hid, width), BF16),
            pltpu.VMEM((e_rows, tok_count), F32),
            pltpu.VMEM((e_rows, tok_count), F32),
            pltpu.VMEM((n_exp * lanes, tok_count), BF16),
            pltpu.VMEM((2, n_exp * cap, width), BF16),
            pltpu.VMEM((2, n_exp * chunk, width), BF16),
            pltpu.VMEM((n_exp * chunk, hid), BF16),
            pltpu.VMEM((n_exp * chunk, hid), BF16),
            pltpu.VMEM((n_exp * chunk, width), BF16),
            pltpu.VMEM((n_exp, nx, cap, width), BF16),
            pltpu.VMEM((n_exp, far, cap, width), BF16),
            pltpu.VMEM((n_exp, far, cap, width), BF16),
            pltpu.VMEM((n_exp, cap, width), F32),
            pltpu.VMEM((n_exp, cap, width), BF16),
            pltpu.VMEM((n_exp * cap, width), BF16),
            pltpu.VMEM((n_dp, n_exp, 8, lanes), F32),
            pltpu.VMEM((n_dp - 1, n_exp, 8, lanes), F32),
            pltpu.VMEM((n_exp, 8, lanes), F32),
            pltpu.VMEM((n_exp, 8, lanes), F32),
            dma((2,)),
            dma((2, n_exp)), dma((2, n_exp)),
            dma((2, n_exp, far)), dma((2, n_exp, far)),
            dma((2, n_exp, nx)), dma((2, n_exp, nx)),
            dma((n_exp, nx)), dma((n_exp, nx)),
            dma((n_exp, far)), dma((n_exp, far)),
            dma((n_exp,)), dma((n_exp,)),
            dma((n_dp - 1,)), dma((n_dp - 1,)),
            dma((n_exp,)), dma((n_exp,)),
        ],
        compiler_params=pltpu.CompilerParams(
            collective_id=0, has_side_effects=True, vmem_limit_bytes=(30 if n_exp <= 4 else 56) * 1024 * 1024
        ),
    )(
        expert_ids.T, gates.T, tokens, cotangent, expert_in[0], expert_out[0]
    )
    return grad_tokens, gate_rows.T, grad_in[None], grad_out[None]


def solution(mesh):
    rows = P(("groups", "expert", "dp"), None)
    return jax.shard_map(
        per_device,
        mesh=mesh,
        in_specs=(rows, rows, rows, rows, P("expert", None, "dp"), P("expert", "dp", None)),
        out_specs=(
            rows,
            rows,
            P(("groups", "expert"), None, "dp"),
            P(("groups", "expert"), "dp", None),
        ),
        check_vma=False,
    )
```

```python
import functools

import jax
import jax.numpy as jnp
from jax import lax
from jax.experimental import pallas as pl
from jax.experimental.pallas import tpu as pltpu
from jax.sharding import PartitionSpec as P

F32 = jnp.float32
BF16 = jnp.bfloat16


def dot(a, b, ca, cb):
    return lax.dot_general(a, b, (((ca,), (cb,)), ((), ())), preferred_element_type=F32)


def split(v):
    hi = v.astype(BF16)
    return hi, (v - hi.astype(F32)).astype(BF16)


def gelu_both(v):
    k = 0.7978845608028654
    v2 = v * v
    t = jnp.tanh(k * v * (1.0 + 0.044715 * v2))
    half = 0.5 + 0.5 * t
    act = v * half
    slope = half + act * (1.0 - t) * (k * (1.0 + 3.0 * 0.044715 * v2))
    return act, slope


def kernel(
    n_exp, n_dp, cap, width, hid,
    ids_ref, gate_ref, tok_ref, cot_ref, win_hbm, wout_hbm,
    gtok_ref, ggate_ref, gin_ref, gout_ref,
    win, wout, hit_s, rank_s, placed, send, buf, h_buf, a_buf,
    part, sib_in, x_out, x_in, own_sum, z_out, back, g_part, g_in, g_out, g_back,
    w_sem, zs, zr, xs, xr, fs, fr, ps, pr, rs, rr, bs, br, gs, gr, ks, kr,
):
    nx = n_dp // 2
    me = lax.axis_index("expert")
    d = lax.axis_index("dp")
    c = d % 2
    x = d // 2
    tok_count = tok_ref.shape[0]
    lanes = placed.shape[1]
    chunk = n_dp * cap

    def exp_dev(e):
        return {"expert": e}

    def dp_dev(i):
        return {"dp": i}

    sib = x * 2 + (1 - c)

    def x_peer(i):
        return ((x + i) % nx) * 2 + c

    def up(s):
        return (me + s) % n_exp

    def down(s):
        return (me + n_exp - s) % n_exp

    def rows(s, who):
        return pl.ds(pl.multiple_of(s * chunk + who * cap, 16), cap)

    def rcopy(src, dst, ss, rsem, dev):
        return pltpu.make_async_remote_copy(
            src_ref=src, dst_ref=dst, send_sem=ss, recv_sem=rsem,
            device_id=dev, device_id_type=pl.DeviceIdType.MESH,
        )

    cw_in = pltpu.make_async_copy(win_hbm, win, w_sem.at[0])
    cw_out = pltpu.make_async_copy(wout_hbm, wout, w_sem.at[1])
    cw_in.start()
    cw_out.start()

    barrier = pltpu.get_barrier_semaphore()

    for s in range(1, n_exp):
        pl.semaphore_signal(barrier, inc=1, device_id=exp_dev(up(s)), device_id_type=pl.DeviceIdType.MESH)
    for i in range(1, n_dp):
        pl.semaphore_signal(
            barrier, inc=1, device_id=dp_dev((d + i) % n_dp), device_id_type=pl.DeviceIdType.MESH
        )

    ids0 = ids_ref[0:1, :]
    ids1 = ids_ref[1:2, :]
    both = gate_ref[...].astype(F32)
    p0 = both[0:1, :]
    p1 = both[1:2, :]
    e_rows = hit_s.shape[0]
    e_iota = lax.broadcasted_iota(jnp.int32, (e_rows, tok_count), 0)
    hit = jnp.where(e_iota == ids0, 1.0, 0.0) + jnp.where(e_iota == ids1, 1.0, 0.0)
    before = jnp.where(
        lax.broadcasted_iota(jnp.int32, (tok_count, tok_count), 0)
        < lax.broadcasted_iota(jnp.int32, (tok_count, tok_count), 1),
        1.0, 0.0,
    )
    rank = dot(hit.astype(BF16), before.astype(BF16), 1, 0)
    slot_iota = lax.broadcasted_iota(jnp.int32, (lanes, tok_count), 0).astype(F32)
    hit_s[...] = hit
    rank_s[...] = rank
    pl.semaphore_wait(barrier, n_exp - 1 + n_dp - 1)

    def z_copy(s, k):
        return rcopy(
            send.at[k, pl.ds(pl.multiple_of(s * cap, 16), cap)], buf.at[k, rows(s, d)],
            zs.at[k, s], zr.at[k, s], exp_dev(up(s)),
        )

    def x_copy(s, k, i):
        return rcopy(
            buf.at[k, rows(s, d)], buf.at[k, rows(s, d)],
            xs.at[k, s, i - 1], xr.at[k, s, i - 1], dp_dev(x_peer(i)),
        )

    def x_landed(s, k, i):
        who = ((x + nx - i) % nx) * 2 + c
        ref = buf.at[k, rows(s, who)]
        return rcopy(ref, ref, xs.at[k, s, i - 1], xr.at[k, s, i - 1], dp_dev(x_peer(i)))

    def f_copy(s, k, i, core):
        ref = buf.at[k, rows(s, ((x + nx - i) % nx) * 2 + core)]
        return rcopy(ref, ref, fs.at[k, s, i], fr.at[k, s, i], dp_dev(sib))

    def fill(s, k):
        e = up(s)
        h_row = hit_s[pl.ds(e, 1), :]
        r_row = rank_s[pl.ds(e, 1), :]
        here = jnp.where(slot_iota == r_row, h_row, 0.0)
        if k == 0:
            placed[pl.ds(pl.multiple_of(s * lanes, 16), lanes), :] = here.astype(BF16)
            return dot(here[:cap].astype(BF16), tok_ref[...], 1, 0).astype(BF16)
        p_row = jnp.where(ids0 == e, p0, p1)
        return dot((here[:cap] * p_row).astype(BF16), cot_ref[...], 1, 0).astype(BF16)

    def start_send(s):
        for k in range(2):
            send[k, pl.ds(pl.multiple_of(s * cap, 16), cap), :] = fill(s, k)
            if unroll and 2 * (s - 1) + k < ahead:
                z_copy(s, k).start()
            elif not unroll:
                pl.when(2 * (s - 1) + k < ahead)(lambda: z_copy(s, k).start())

    def spread(s, k):
        for i in range(1, nx):
            x_copy(s, k, i).start()
        f_copy(s, k, 0, c).start()

    def kick(s, k):
        z_copy(s, k).wait_send()
        later = s + (k + ahead) // 2
        if unroll and later < n_exp:
            z_copy(later, (k + ahead) % 2).start()
        elif not unroll:
            pl.when(later < n_exp)(lambda: z_copy(later, (k + ahead) % 2).start())

    def f1(s):
        for k in range(2):
            kick(s, k)
            z_copy(s, k).wait_recv()
            spread(s, k)

    def f2(s):
        for k in range(2):
            for i in range(1, nx):
                x_landed(s, k, i).wait_recv()
                f_copy(s, k, i, c).start()

    def p_copy(s, i):
        who = ((x + i) % nx) * 2 + (1 - c)
        return rcopy(
            part.at[rows(s, who)], sib_in.at[s, i], ps.at[s, i], pr.at[s, i], dp_dev(sib)
        )

    def compute(s):
        for k in range(2):
            for i in range(nx):
                f_copy(s, k, i, 1 - c).wait_recv()
        here = pl.ds(pl.multiple_of(s * chunk, 16), chunk)
        pre = dot(buf[0, here, :], win[...], 1, 0)
        grad_act = dot(buf[1, here, :], wout[...], 1, 1)
        act, slope = gelu_both(pre)
        hidden = (grad_act * slope).astype(BF16)
        h_buf[here, :] = hidden
        a_buf[here, :] = act.astype(BF16)
        part[here, :] = dot(hidden, win[...], 1, 1).astype(BF16)
        for i in range(nx):
            p_copy(s, i).start()
        hi, lo = split(act * grad_act)
        ones = jnp.ones((8, hid), BF16)
        for i in range(n_dp):
            own = slice(i * cap, (i + 1) * cap)
            g_part[i, s, :, 0:cap] = dot(ones, hi[own], 1, 1) + dot(ones, lo[own], 1, 1)

    def r_copy(s, i):
        return rcopy(
            x_out.at[s, i - 1], x_in.at[s, i - 1], rs.at[s, i - 1], rr.at[s, i - 1], dp_dev(x_peer(i))
        )

    def r1(s):
        for i in list(range(1, nx)) + [0]:
            p_copy(s, i).wait_recv()
            who = ((x + i) % nx) * 2 + c
            total = part[rows(s, who), :].astype(F32) + sib_in[s, i].astype(F32)
            if i == 0:
                own_sum[s] = total
            else:
                x_out[s, i - 1] = total.astype(BF16)
                r_copy(s, i).start()

    def b_copy(s):
        return rcopy(
            z_out.at[s], back.at[pl.ds(pl.multiple_of(s * cap, 16), cap)],
            bs.at[s], br.at[s], exp_dev(down(s)),
        )

    def r2(s):
        total = own_sum[s]
        for i in range(1, nx):
            r_copy(s, i).wait_recv()
            total += x_in[s, i - 1].astype(F32)
        return total.astype(BF16)

    def r2_send(s):
        z_out[s] = r2(s)
        b_copy(s).start()

    def g_copy(i):
        return rcopy(
            g_part.at[(d + i) % n_dp], g_in.at[i - 1], gs.at[i - 1], gr.at[i - 1],
            dp_dev((d + i) % n_dp),
        )

    def k_copy(s):
        return rcopy(g_out.at[s], g_back.at[s], ks.at[s], kr.at[s], exp_dev(down(s)))

    g_part[...] = jnp.zeros_like(g_part)
    unroll = n_exp == 4
    ahead = 1

    def over(low, high, body):
        if unroll:
            for s in range(low, high):
                body(s)
        else:
            lax.fori_loop(low, high, lambda s, t: (body(s), t)[1], 0)

    start_send(1)
    for k in range(2):
        buf[k, rows(0, d), :] = fill(0, k)
        spread(0, k)
    over(2, n_exp, start_send)
    cw_in.wait()
    cw_out.wait()

    if unroll:
        f1(1)
        f2(0)
        f1(2)
        f2(1)
        compute(0)
        f1(3)
        f2(2)
        compute(1)
        r1(0)
        compute(2)
        r1(1)
        back[0:cap, :] = r2(0)
    else:
        f1(1)
        f2(0)
        compute(0)
        f1(2)
        f2(1)
        compute(1)
        r1(0)
        f1(3)
        f2(2)
        compute(2)
        r1(1)
        back[0:cap, :] = r2(0)

        def steady(t):
            f1(t)
            f2(t - 1)
            compute(t - 1)
            r1(t - 2)
            r2_send(t - 3)

        over(4, n_exp, steady)
    last = n_exp - 1
    f2(last)
    compute(last)
    for i in range(1, n_dp):
        g_copy(i).start()
    r1(last - 1)
    r2_send(last - 2)
    tile = 256

    def in_tile(j, t):
        cols = pl.ds(pl.multiple_of(j * tile, tile), tile)
        gin_ref[cols, :] = dot(buf[0, :, cols], h_buf[...], 0, 0).astype(BF16)
        return t

    def out_tile(j, t):
        cols = pl.ds(pl.multiple_of(j * tile, tile), tile)
        gout_ref[:, cols] = dot(a_buf[...], buf[1, :, cols], 0, 0).astype(BF16)
        return t

    r1(last)
    r2_send(last - 1)
    lax.fori_loop(0, width // tile, in_tile, 0)
    r2_send(last)
    g_sum = g_part[d]
    for i in range(1, n_dp):
        g_copy(i).wait_recv()
        g_sum += g_in[i - 1]
    g_out[...] = g_sum
    over(1, n_exp, lambda s: k_copy(s).start())
    lax.fori_loop(0, width // tile, out_tile, 0)
    g_back[0] = g_out[0]
    over(1, n_exp, lambda s: k_copy(s).wait_recv())
    gate0 = jnp.zeros((8, tok_count), F32)
    gate1 = jnp.zeros((8, tok_count), F32)
    for s in range(n_exp):
        hi, lo = split(g_back[s])
        mine = placed[s * lanes : (s + 1) * lanes, :]
        value = dot(hi, mine, 1, 0) + dot(lo, mine, 1, 0)
        gate0 += jnp.where(ids0 == up(s), value, 0.0)
        gate1 += jnp.where(ids1 == up(s), value, 0.0)
    first = lax.broadcasted_iota(jnp.int32, (2, tok_count), 0) == 0
    ggate_ref[...] = jnp.where(first, gate0[0:2] / p0, gate1[0:2] / p1).astype(BF16)

    over(1, n_exp, lambda s: b_copy(s).wait_recv())
    total = jnp.zeros((tok_count, width), F32)
    for s in range(n_exp):
        total += dot(
            placed[s * lanes : s * lanes + cap, :], back[s * cap : (s + 1) * cap, :], 0, 0
        )
    gtok_ref[...] = total.astype(BF16)

    def drain(s):
        b_copy(s).wait_send()
        k_copy(s).wait_send()

    def drain_all(s):
        for k in range(2):
            for i in range(1, nx):
                x_copy(s, k, i).wait_send()
            for i in range(nx):
                f_copy(s, k, i, c).wait_send()
        for i in range(nx):
            p_copy(s, i).wait_send()
        for i in range(1, nx):
            r_copy(s, i).wait_send()

    over(1, n_exp, drain)
    over(0, n_exp, drain_all)
    for i in range(1, n_dp):
        g_copy(i).wait_send()


def per_device(tokens, cotangent, expert_ids, gates, expert_in, expert_out):
    tok_count, width = tokens.shape
    n_exp = lax.axis_size("expert")
    n_dp = lax.axis_size("dp")
    nx = n_dp // 2
    hid = expert_in.shape[2]
    cap = (5 * tok_count + 2 * n_exp - 1) // (2 * n_exp)
    cap = (cap + 15) // 16 * 16
    chunk = n_dp * cap
    lanes = 128
    e_rows = (n_exp + 15) // 16 * 16
    vmem = pl.BlockSpec(memory_space=pltpu.VMEM)
    hbm = pl.BlockSpec(memory_space=pltpu.HBM)
    dma = pltpu.SemaphoreType.DMA
    far = max(nx - 1, 1)
    grad_tokens, gate_rows, grad_in, grad_out = pl.pallas_call(
        functools.partial(kernel, n_exp, n_dp, cap, width, hid),
        out_shape=(
            jax.ShapeDtypeStruct((tok_count, width), BF16),
            jax.ShapeDtypeStruct((2, tok_count), BF16),
            jax.ShapeDtypeStruct((width, hid), BF16),
            jax.ShapeDtypeStruct((hid, width), BF16),
        ),
        in_specs=[vmem] * 4 + [hbm] * 2,
        out_specs=(vmem,) * 4,
        scratch_shapes=[
            pltpu.VMEM((width, hid), BF16),
            pltpu.VMEM((hid, width), BF16),
            pltpu.VMEM((e_rows, tok_count), F32),
            pltpu.VMEM((e_rows, tok_count), F32),
            pltpu.VMEM((n_exp * lanes, tok_count), BF16),
            pltpu.VMEM((2, n_exp * cap, width), BF16),
            pltpu.VMEM((2, n_exp * chunk, width), BF16),
            pltpu.VMEM((n_exp * chunk, hid), BF16),
            pltpu.VMEM((n_exp * chunk, hid), BF16),
            pltpu.VMEM((n_exp * chunk, width), BF16),
            pltpu.VMEM((n_exp, nx, cap, width), BF16),
            pltpu.VMEM((n_exp, far, cap, width), BF16),
            pltpu.VMEM((n_exp, far, cap, width), BF16),
            pltpu.VMEM((n_exp, cap, width), F32),
            pltpu.VMEM((n_exp, cap, width), BF16),
            pltpu.VMEM((n_exp * cap, width), BF16),
            pltpu.VMEM((n_dp, n_exp, 8, lanes), F32),
            pltpu.VMEM((n_dp - 1, n_exp, 8, lanes), F32),
            pltpu.VMEM((n_exp, 8, lanes), F32),
            pltpu.VMEM((n_exp, 8, lanes), F32),
            dma((2,)),
            dma((2, n_exp)), dma((2, n_exp)),
            dma((2, n_exp, far)), dma((2, n_exp, far)),
            dma((2, n_exp, nx)), dma((2, n_exp, nx)),
            dma((n_exp, nx)), dma((n_exp, nx)),
            dma((n_exp, far)), dma((n_exp, far)),
            dma((n_exp,)), dma((n_exp,)),
            dma((n_dp - 1,)), dma((n_dp - 1,)),
            dma((n_exp,)), dma((n_exp,)),
        ],
        compiler_params=pltpu.CompilerParams(
            collective_id=0, has_side_effects=True, vmem_limit_bytes=58 * 1024 * 1024
        ),
    )(
        expert_ids.T, gates.T, tokens, cotangent, expert_in[0], expert_out[0]
    )
    return grad_tokens, gate_rows.T, grad_in[None], grad_out[None]


def solution(mesh):
    rows = P(("groups", "expert", "dp"), None)
    return jax.shard_map(
        per_device,
        mesh=mesh,
        in_specs=(rows, rows, rows, rows, P("expert", None, "dp"), P("expert", "dp", None)),
        out_specs=(
            rows,
            rows,
            P(("groups", "expert"), None, "dp"),
            P(("groups", "expert"), "dp", None),
        ),
        check_vma=False,
    )
```
